256 devices in a mesh: terms: 8 (over x, z_lo), row: 4 (over y), col: 8 (over z_hi, core).
Axes of the slice: x: 4, y: 4, z: 8 (z_hi: 4, z_lo: 2; z = z_hi * 2 + z_lo), core: 2. Of those that a mesh axis runs over, the one named last changes fastest.
Arguments:
- psi: bfloat16 [2048, 2048], P('row', 'col'), may hold values from -6 to 6
- left_ops: bfloat16 [24, 2048, 2048], P('terms', 'row', 'col')
- right_ops_t: bfloat16 [24, 2048, 2048], P('terms', 'row', 'col')
- term_count: int32 [8], P('terms'), may hold values from 1 to 3, as said below
Outputs:
- sigma: bfloat16 [2048, 2048], P('row', 'col')
- residual: bfloat16 [2048, 2048], P('row', 'col')
- energy: float32 [], replicated
The draws below stay inside these ranges and needn't reach their ends.
Inputs may be any that keep to these rules, and one draw needn't show every extreme that they name: Group g uses its first term_count[g] slots and ignores the others; some group uses all 3, another uses one.
All inputs are finite; a program needn't handle non-finite values.
Results may differ from the reference program's by a relative error of at most 0.0056.
Values may be sent and summed in bfloat16 or wider, within the bound.
No kernel may reach another device: no remote copies, remote signals or barrier semaphores. Data moves between devices by JAX's collectives and lax.ppermute only.
A program may use at most 64 MiB of HBM per device.

```python
import jax
import jax.numpy as jnp
from jax import lax

SECTOR = 2048
TERM_SLOTS = 3
GROUPS = 8


def diagonal_mask():
    rows = jnp.arange(SECTOR, dtype=jnp.int32)[:, None]
    cols = jnp.arange(SECTOR, dtype=jnp.int32)[None, :]
    return (rows == cols)[None, :, :]


def draw_left_ops(key, part):
    key = jax.random.fold_in(key, 11)
    key_off, key_diag = jax.random.split(key)
    shape = (GROUPS * TERM_SLOTS, SECTOR, SECTOR)
    off = jax.random.normal(key_off, shape, jnp.float32)
    diag = jax.random.uniform(key_diag, shape, jnp.float32, 0.5, 1.5)
    values = off * SECTOR ** (-0.5)
    return jnp.where(diagonal_mask(), diag, values).astype(jnp.bfloat16)


def draw_right_ops_t(key, part):
    key = jax.random.fold_in(key, 23)
    key_off, key_diag = jax.random.split(key)
    shape = (GROUPS * TERM_SLOTS, SECTOR, SECTOR)
    off = jax.random.normal(key_off, shape, jnp.float32)
    diag = jax.random.uniform(key_diag, shape, jnp.float32, 0.5, 1.5)
    values = off * SECTOR ** (-0.5)
    return jnp.where(diagonal_mask(), diag, values).astype(jnp.bfloat16)


def draw_term_count(key, part):
    key = jax.random.fold_in(key, 37)
    key_count, key_pick, key_other = jax.random.split(key, 3)
    counts = jax.random.randint(key_count, (GROUPS,), 1, TERM_SLOTS + 1, jnp.int32)
    chosen = jax.random.randint(key_pick, (), 0, GROUPS, jnp.int32)
    offset = jax.random.randint(key_other, (), 1, GROUPS, jnp.int32)
    lightest = (chosen + offset) % GROUPS
    places = jnp.arange(GROUPS, dtype=jnp.int32)
    counts = jnp.where(places == lightest, jnp.int32(1), counts)
    return jnp.where(places == chosen, jnp.int32(TERM_SLOTS), counts)


def steps_of(stream_key, dims, cuts, least, largest):
    gain = 1.0
    for dim, shards_of in cuts:
        draws = jax.random.uniform(jax.random.fold_in(jax.random.fold_in(stream_key, 6), dim), (shards_of,), jnp.float32, least / len(cuts), largest / len(cuts))
        gain = gain * jnp.repeat(jnp.exp(draws), dims[dim] // shards_of).reshape((-1,) + (1,) * (len(dims) - 1 - dim))
    return gain


def scatter_about(stream_key, dims, deviation, reach, shards=(), held_as=jnp.bfloat16):
    entries = jax.random.normal(stream_key, dims, jnp.float32) * deviation
    if len(shards) > 0:
        entries = steps_of(stream_key, dims, shards, -0.22, 0.18) * entries
    return jnp.clip(entries, min=-reach, max=reach).astype(held_as)


def setup_inputs(seed: int = 0) -> dict:
    streams_of = jax.random.split(jax.random.key(seed), 5)
    return {
        "psi": scatter_about(streams_of[0], (SECTOR, SECTOR), 1.0, 6.0, ((0, 4), (1, 8))),
        "left_ops": draw_left_ops(jax.random.fold_in(streams_of[4], 71), 0),
        "right_ops_t": draw_right_ops_t(jax.random.fold_in(streams_of[4], 71), 0),
        "term_count": draw_term_count(jax.random.fold_in(streams_of[4], 71), 0),
    }


def reference(psi, left_ops, right_ops_t, term_count):
    total_slots = GROUPS * TERM_SLOTS
    slot_of = jnp.arange(total_slots, dtype=jnp.int32) % TERM_SLOTS
    live = slot_of < jnp.repeat(term_count, TERM_SLOTS, total_repeat_length=total_slots)

    def step(total, item):
        left, right, flag = item
        mixed = jnp.dot(left, psi, preferred_element_type=jnp.float32).astype(jnp.bfloat16)
        term = jnp.dot(mixed, right, preferred_element_type=jnp.float32)
        return total + jnp.where(flag, term, jnp.float32(0.0)), None

    start = jnp.zeros((SECTOR, SECTOR), jnp.float32)
    sigma_full, _ = lax.scan(step, start, (left_ops, right_ops_t, live))
    psi_wide = psi.astype(jnp.float32)
    energy = jnp.sum(psi_wide * sigma_full) / jnp.sum(psi_wide * psi_wide)
    residual = (sigma_full - energy * psi_wide).astype(jnp.bfloat16)
    return sigma_full.astype(jnp.bfloat16), residual, energy
```

```python
import jax
import jax.numpy as jnp
from jax import lax
from jax.experimental import pallas as pl
from jax.experimental.pallas import tpu as pltpu
from jax.sharding import Mesh, PartitionSpec as P

TERMS = ("x", "zlo")
BF16, F32 = jnp.bfloat16, jnp.float32
ANY = pl.BlockSpec(memory_space=pl.ANY)
SMEM = pl.BlockSpec(memory_space=pltpu.SMEM)
VMEM = pl.BlockSpec(memory_space=pltpu.VMEM)


def shift(x, axis, n, k):
    return lax.ppermute(x, axis, [(i, (i + k) % n) for i in range(n)])


def gather(x, axis, dim):
    half = x.shape[dim] // 2
    before = shift(x, axis, 4, 1)
    after = shift(x, axis, 4, 3)
    low = shift(lax.slice_in_dim(before, 0, half, axis=dim), axis, 4, 1)
    high = shift(lax.slice_in_dim(after, half, 2 * half, axis=dim), axis, 4, 3)
    return after, low, high, before


def first_kernel(place, own, sib, r0, r1, r2a, r2b, r3, keep, send, psi_buf, r_buf, sems):
    m, l, c = place[0], place[1], place[2]
    copies = [
        pltpu.make_async_copy(own, psi_buf.at[c], sems.at[0]),
        pltpu.make_async_copy(sib, psi_buf.at[1 - c], sems.at[1]),
        pltpu.make_async_copy(r0, r_buf.at[0], sems.at[2]),
        pltpu.make_async_copy(r1, r_buf.at[1], sems.at[3]),
        pltpu.make_async_copy(r2a, r_buf.at[2, :, pl.ds(0, 256)], sems.at[4]),
        pltpu.make_async_copy(r2b, r_buf.at[2, :, pl.ds(256, 256)], sems.at[5]),
        pltpu.make_async_copy(r3, r_buf.at[3], sems.at[6]),
    ]
    for copy in copies:
        copy.start()
    for copy in copies:
        copy.wait()
    for s in range(3):
        for out, half in ((keep, c), (send, 1 - c)):
            total = jnp.zeros((256, 256), F32)
            for d in range(4):
                e = lax.rem(m + d - l + 4, 4)
                rows = pl.ds(pl.multiple_of(e * 512 + half * 256, 256), 256)
                for h in range(2):
                    total += jnp.dot(
                        psi_buf[h, rows, :],
                        r_buf[d, s, h * 256 : (h + 1) * 256, :],
                        preferred_element_type=F32,
                    )
            out[s] = total.astype(BF16)


def second_kernel(place, l0, l1, l2a, l2b, l3, w0, w1, w2a, w2b, w3, own, sib, mine, theirs, dots, l_buf, w_buf, psi_buf, sems):
    m, l, live = place[0], place[1], place[3]
    copies = [
        pltpu.make_async_copy(l0, l_buf.at[0], sems.at[0]),
        pltpu.make_async_copy(l1, l_buf.at[1], sems.at[1]),
        pltpu.make_async_copy(l2a, l_buf.at[2, :, pl.ds(0, 256)], sems.at[2]),
        pltpu.make_async_copy(l2b, l_buf.at[2, :, pl.ds(256, 256)], sems.at[3]),
        pltpu.make_async_copy(l3, l_buf.at[3], sems.at[4]),
        pltpu.make_async_copy(w0, w_buf.at[0], sems.at[5]),
        pltpu.make_async_copy(w1, w_buf.at[1], sems.at[6]),
        pltpu.make_async_copy(w2a, w_buf.at[2, :, :, pl.ds(0, 128)], sems.at[7]),
        pltpu.make_async_copy(w2b, w_buf.at[2, :, :, pl.ds(128, 128)], sems.at[8]),
        pltpu.make_async_copy(w3, w_buf.at[3], sems.at[9]),
        pltpu.make_async_copy(own.at[pl.ds(0, 512)], psi_buf.at[0], sems.at[10]),
        pltpu.make_async_copy(sib.at[pl.ds(0, 512)], psi_buf.at[1], sems.at[11]),
    ]
    for copy in copies:
        copy.start()
    for copy in copies:
        copy.wait()
    above = jnp.zeros((8, 256), F32)
    for h, out in ((0, mine), (1, theirs)):
        for block in range(2):
            rows = slice(block * 256, (block + 1) * 256)
            out[rows] = jnp.zeros((256, 256), F32)
            for s in range(3):

                @pl.when(s < live)
                def _(s=s, h=h, rows=rows, out=out):
                    total = out[rows]
                    for e in range(4):
                        d = lax.rem(l + e - m + 4, 4)
                        total += jnp.dot(
                            l_buf[e, s, rows, :], w_buf[d, h, s], preferred_element_type=F32
                        )
                    out[rows] = total

            product = out[rows] * psi_buf[h, rows, :].astype(F32)
            above += product.reshape(32, 8, 256).sum(0)
    wide = psi_buf[0].astype(F32)
    below = (wide * wide).reshape(64, 8, 256).sum(0)
    dots[0:8] = above
    dots[8:16] = below


def per_device(psi, left_ops, right_ops_t, term_count):
    m, l, c = lax.axis_index("row"), lax.axis_index("zhi"), lax.axis_index("core")
    place = jnp.stack([m, l, c, term_count[0]]).astype(jnp.int32)

    p1, p2a, p2b, p3 = gather(psi, "zhi", 0)
    own = jnp.concatenate([psi, p1, p2a, p2b, p3], axis=0)
    sib = shift(own, "core", 2, 1)

    r1, r2a, r2b, r3 = gather(right_ops_t, "row", 1)
    left, _ = lax.optimization_barrier((left_ops, p3))
    l1, l2a, l2b, l3 = gather(left, "zhi", 1)

    keep, send = pl.pallas_call(
        first_kernel,
        out_shape=[jax.ShapeDtypeStruct((3, 256, 256), BF16)] * 2,
        in_specs=[SMEM] + [ANY] * 7,
        out_specs=[VMEM] * 2,
        scratch_shapes=[
            pltpu.VMEM((2, 2048, 256), BF16),
            pltpu.VMEM((4, 3, 512, 256), BF16),
            pltpu.SemaphoreType.DMA((7,)),
        ],
        compiler_params=pltpu.CompilerParams(vmem_limit_bytes=24 << 20),
        cost_estimate=pl.CostEstimate(flops=3 * 2 * 512 * 2048 * 256, bytes_accessed=6 << 20, transcendentals=0),
    )(place, own, sib, right_ops_t, r1, r2a, r2b, r3)

    w = jnp.stack([keep, shift(send, "core", 2, 1)])
    w1, w2a, w2b, w3 = gather(w, "row", 2)

    mine, theirs, dots = pl.pallas_call(
        second_kernel,
        out_shape=[jax.ShapeDtypeStruct((512, 256), F32)] * 2 + [jax.ShapeDtypeStruct((16, 256), F32)],
        in_specs=[SMEM] + [ANY] * 12,
        out_specs=[VMEM] * 3,
        scratch_shapes=[
            pltpu.VMEM((4, 3, 512, 256), BF16),
            pltpu.VMEM((4, 2, 3, 256, 256), BF16),
            pltpu.VMEM((2, 512, 256), BF16),
            pltpu.SemaphoreType.DMA((12,)),
        ],
        compiler_params=pltpu.CompilerParams(vmem_limit_bytes=24 << 20),
        cost_estimate=pl.CostEstimate(flops=3 * 2 * 512 * 1024 * 512, bytes_accessed=8 << 20, transcendentals=0),
    )(place, left_ops, l1, l2a, l2b, l3, w, w1, w2a, w2b, w3, own, sib)

    partial = mine + shift(theirs, "core", 2, 1)
    sums = jnp.stack([dots[:8].sum(), dots[8:].sum()])
    sums = jnp.broadcast_to(jnp.pad(sums, (0, 6))[:, None], (8, 256))
    payload = jnp.concatenate(
        [partial.reshape(8, 64, 256), jnp.broadcast_to(sums, (8, 8, 256))], axis=1
    )
    reduced = lax.all_to_all(payload, TERMS, 0, 0, tiled=True).sum(0)
    chunk, sums = reduced[:64], reduced[64:, :128]
    sums = sums + shift(sums, "row", 4, 1) + shift(sums, "row", 4, 2) + shift(sums, "row", 4, 3)
    sigma_full = lax.all_to_all(
        jnp.broadcast_to(chunk, (8, 64, 256)), TERMS, 0, 0, tiled=True
    ).reshape(512, 256)
    sums = sums + shift(sums, "zhi", 4, 1) + shift(sums, "zhi", 4, 2) + shift(sums, "zhi", 4, 3)
    sums = sums + shift(sums, "core", 2, 1)
    energy = sums[0, 0] / (sums[1, 0] * F32(0.125))
    residual = (sigma_full - energy * psi.astype(F32)).astype(BF16)
    return sigma_full.astype(BF16), residual, energy


def solution(mesh):
    fine = Mesh(mesh.devices.reshape(4, 2, 4, 4, 2), ("x", "zlo", "row", "zhi", "core"))
    col = ("zhi", "core")
    in_specs = (P("row", col), P(TERMS, "row", col), P(TERMS, "row", col), P(TERMS))
    out_specs = (P("row", col), P("row", col), P())
    return jax.shard_map(
        per_device, mesh=fine, in_specs=in_specs, out_specs=out_specs, check_vma=False
    )
```

```python
import jax
import jax.numpy as jnp
from jax import lax
from jax.experimental import pallas as pl
from jax.experimental.pallas import tpu as pltpu
from jax.sharding import Mesh, PartitionSpec as P

TERMS = ("x", "zlo")
BF16, F32 = jnp.bfloat16, jnp.float32
SMEM = pl.BlockSpec(memory_space=pltpu.SMEM)
VMEM = pl.BlockSpec(memory_space=pltpu.VMEM)
HBM = pl.BlockSpec(memory_space=pl.ANY)


def shift(x, axis, n, k):
    return lax.ppermute(x, axis, [(i, (i + k) % n) for i in range(n)])


def fetch(x):
    pairs = []
    for t in range(8):
        for at in range(16):
            for c in range(2):
                source = (at + 2 * t + c) % 16
                pairs.append((t * 32 + source * 2 + c, t * 32 + at * 2 + c))
    return lax.ppermute(x, (*TERMS, "row", "zhi", "core"), pairs)


def together(*xs):
    return lax.optimization_barrier(xs)


def far(after, before, axis, dim):
    half = after.shape[dim] // 2
    low = shift(lax.slice_in_dim(before, 0, half, axis=dim), axis, 4, 1)
    high = shift(lax.slice_in_dim(after, half, 2 * half, axis=dim), axis, 4, 3)
    return low, high


def spread_to(x, axis):
    n = 4
    return lax.all_to_all(jnp.broadcast_to(x[None], (n, *x.shape)), axis, 0, 0, tiled=True)


def start(moves, sems):
    copies = [pltpu.make_async_copy(a, b, sems.at[i]) for i, (a, b) in enumerate(moves)]
    for copy in copies:
        copy.start()
    return copies


def wait(copies):
    for copy in copies:
        copy.wait()


def first_kernel(place, own, sib, r0, r1, r2a, r2b, r3, keep, send, psi, right, sems):
    m, c = place[0], place[2]
    first = start([(own, psi.at[c]), (sib, psi.at[1 - c])], sems.at[3])
    slots = []
    for s in range(3):
        moves = [(r0.at[s], right.at[0, s]), (r1.at[s], right.at[1, s]), (r3.at[s], right.at[3, s])]
        moves += [(r2a.at[s], right.at[2, s, pl.ds(0, 256)]), (r2b.at[s], right.at[2, s, pl.ds(256, 256)])]
        slots.append(start(moves, sems.at[s]))
    wait(first)
    for s in range(3):
        wait(slots[s])
        for out, part in ((keep, c), (send, 1 - c)):
            total = jnp.zeros((256, 256), F32)
            for d in range(4):
                j = lax.rem(m + d, 4)
                for h in range(2):
                    rows = jnp.concatenate([psi[h, 2 * part, j], psi[h, 2 * part + 1, j]], axis=0)
                    total += jnp.dot(
                        rows, right[d, s, h * 256 : (h + 1) * 256], preferred_element_type=F32
                    )
            out[s] = total.astype(BF16)


def split(x):
    high = x.astype(BF16)
    return [high, (x - high.astype(F32)).astype(BF16)]


def second_kernel(place, left, w0, w1, w2a, w2b, w3, own, sib, out, total, l_buf, w_buf, psi, sems):
    m, l, c, live = place[0], place[1], place[2], place[4]
    slots = []
    for s in range(3):
        moves = [(left.at[:, s], l_buf.at[:, s]), (w0.at[:, s], w_buf.at[0, :, s]), (w1.at[:, s], w_buf.at[1, :, s])]
        moves += [(w2a.at[s], w_buf.at[2, 0, s]), (w2b.at[s], w_buf.at[2, 1, s]), (w3.at[:, s], w_buf.at[3, :, s])]
        slots.append(start(moves, sems.at[s]))
    last = start([(own.at[:, l], psi.at[0]), (sib.at[:, l], psi.at[1])], sems.at[3])
    for s in range(3):
        wait(slots[s])

        @pl.when(s < live)
        def _(s=s):
            for block in range(2):
                rows = slice(block * 256, (block + 1) * 256)
                for h in range(2):
                    term = jnp.zeros((256, 256), F32) if s == 0 else total[h, rows]
                    for d in range(4):
                        term += jnp.dot(
                            l_buf[lax.rem(m + d, 4), s, rows, :], w_buf[d, h, s], preferred_element_type=F32
                        )
                    total[h, rows] = term

    wait(last)
    above, below = jnp.zeros((8, 256), F32), jnp.zeros((8, 256), F32)
    for part in range(8):
        for h in range(2):
            wide = psi[h, part // 2, (part % 2) * 64 : (part % 2) * 64 + 64].astype(F32)
            term = total[h, part * 64 : (part + 1) * 64]
            above += (wide * term).reshape(8, 8, 256).sum(0)
            if h == 0:
                below += (wide * wide).reshape(8, 8, 256).sum(0)
            out[2 * part + (c if h == 0 else 1 - c), 0:64] = term.astype(BF16)
    sums = [y for x in (above, below) for y in split(x.reshape(4, 2, 256).sum(0).reshape(2, 256))]
    sums = jnp.concatenate(sums + [jnp.zeros((8, 256), BF16)], axis=0)
    for part in range(16):
        out[part, 64:80] = sums


def third_kernel(parts, out, sums):
    chunk = parts[0].astype(F32)
    for part in range(1, 16):
        chunk += parts[part].astype(F32)
    out[...] = chunk[0:64]
    for i in range(2):
        one = chunk[64 + 4 * i : 68 + 4 * i].sum(0, keepdims=True).sum(1, keepdims=True)
        sums[i : i + 1] = jnp.broadcast_to(one, (1, 128))
    sums[2:8] = jnp.zeros((6, 128), F32)


def spread_kernel(chunk, one, other, out):
    for part in range(8):
        out[part, 0:64] = chunk[...]
        out[part, 64:72, 0:128] = one[...]
        out[part, 64:72, 128:256] = other[...]


def last_kernel(parts, psi, sigma, residual, energy):
    tail = parts[0, 64:72]
    for part in range(1, 8):
        tail += parts[part, 64:72]
    tail = tail[:, 0:128] + tail[:, 128:256]
    ratio = jnp.broadcast_to(tail[0:1] / (tail[1:2] * 0.125), (8, 128))
    energy[...] = ratio
    row = jnp.concatenate([ratio[0:1], ratio[0:1]], axis=1)
    for part in range(8):
        rows = slice(part * 64, (part + 1) * 64)
        full = parts[part, 0:64]
        sigma[rows] = full.astype(BF16)
        residual[rows] = (full - row * psi[rows].astype(F32)).astype(BF16)


def call(kernel, outs, ins, *args, scratch=(), limit=8, flops=0, nbytes=1 << 10):
    return pl.pallas_call(
        kernel,
        out_shape=[jax.ShapeDtypeStruct(shape, dtype) for shape, dtype in outs],
        in_specs=ins,
        out_specs=[VMEM] * len(outs),
        scratch_shapes=scratch,
        compiler_params=pltpu.CompilerParams(vmem_limit_bytes=limit << 20),
        cost_estimate=pl.CostEstimate(flops=flops, bytes_accessed=nbytes, transcendentals=0),
    )(*args)


def per_device(psi, left_ops, right_ops_t, term_count):
    m, l, c = lax.axis_index("row"), lax.axis_index("zhi"), lax.axis_index("core")
    a = lax.axis_index("x")
    place = jnp.stack([m, l, c, a, term_count[0]]).astype(jnp.int32)

    left = lax.all_gather(left_ops, "zhi")

    quarter = lax.dynamic_slice_in_dim(psi, a * 128, 128, 0)
    r1, r3 = shift(right_ops_t, "row", 4, 3), shift(right_ops_t, "row", 4, 1)
    column = spread_to(quarter, "zhi")
    column, r1, r3 = together(column, r1, r3)
    r2a, r2b = far(r1, r3, "row", 1)
    own = spread_to(column, "x")
    own, r2a, r2b = together(own, r2a, r2b)
    sib = shift(own, "core", 2, 1)
    keep, send = call(
        first_kernel, [((3, 256, 256), BF16)] * 2, [SMEM] + [HBM] * 7,
        place, own, sib, right_ops_t, r1, r2a, r2b, r3,
        scratch=[pltpu.VMEM((2, 4, 4, 128, 256), BF16), pltpu.VMEM((4, 3, 512, 256), BF16), pltpu.SemaphoreType.DMA((4, 5))],
        limit=56,
    )
    w = jnp.stack([keep, shift(send, "core", 2, 1)])
    w1, w3 = shift(w, "row", 4, 3), shift(w, "row", 4, 1)
    w2a = shift(w3[0], "row", 4, 1)
    w2b = shift(w1[1], "row", 4, 3)

    (payload,) = call(
        second_kernel, [((16, 80, 256), BF16)], [SMEM] + [HBM] * 8,
        place, left, w, w1, w2a, w2b, w3, own, sib,
        scratch=[
            pltpu.VMEM((2, 512, 256), F32), pltpu.VMEM((4, 3, 512, 256), BF16), pltpu.VMEM((4, 2, 3, 256, 256), BF16),
            pltpu.VMEM((2, 4, 128, 256), BF16), pltpu.SemaphoreType.DMA((4, 6)),
        ],
        limit=56,
    )

    parts = lax.all_to_all(payload, (*TERMS, "core"), 0, 0, tiled=True)
    chunk, sums = call(third_kernel, [((64, 256), F32), ((8, 128), F32)], [VMEM], parts)
    one = fetch(sums)
    other = shift(one, "core", 2, 1)
    (spread,) = call(spread_kernel, [((8, 72, 256), F32)], [VMEM] * 3, chunk, one, other)
    full = lax.all_to_all(spread, TERMS, 0, 0, tiled=True)
    sigma, residual, energy = call(
        last_kernel, [((512, 256), BF16), ((512, 256), BF16), ((8, 128), F32)], [VMEM] * 2, full, psi
    )
    return sigma, residual, energy[0, 0]


def solution(mesh):
    fine = Mesh(mesh.devices.reshape(4, 2, 4, 4, 2), ("x", "zlo", "row", "zhi", "core"))
    col = ("zhi", "core")
    in_specs = (P("row", col), P(TERMS, "row", col), P(TERMS, "row", col), P(TERMS))
    out_specs = (P("row", col), P("row", col), P())
    return jax.shard_map(
        per_device, mesh=fine, in_specs=in_specs, out_specs=out_specs, check_vma=False
    )
```

```python
import jax
import jax.numpy as jnp
from jax import lax
from jax.experimental import pallas as pl
from jax.experimental.pallas import tpu as pltpu
from jax.sharding import Mesh, PartitionSpec as P

TERMS = ("x", "zlo")
BF16, F32 = jnp.bfloat16, jnp.float32
SMEM = pl.BlockSpec(memory_space=pltpu.SMEM)
VMEM = pl.BlockSpec(memory_space=pltpu.VMEM)
HBM = pl.BlockSpec(memory_space=pl.ANY)


def shift(x, axis, n, k):
    return lax.ppermute(x, axis, [(i, (i + k) % n) for i in range(n)])


def fetch(x):
    pairs = []
    for t in range(8):
        for at in range(16):
            for c in range(2):
                source = (at + 2 * t + c) % 16
                pairs.append((t * 32 + source * 2 + c, t * 32 + at * 2 + c))
    return lax.ppermute(x, (*TERMS, "row", "zhi", "core"), pairs)


def together(*xs):
    return lax.optimization_barrier(xs)


def far(after, before, axis, dim):
    half = after.shape[dim] // 2
    low = shift(lax.slice_in_dim(before, 0, half, axis=dim), axis, 4, 1)
    high = shift(lax.slice_in_dim(after, half, 2 * half, axis=dim), axis, 4, 3)
    return low, high


def spread_to(x, axis):
    n = 4
    return lax.all_to_all(jnp.broadcast_to(x[None], (n, *x.shape)), axis, 0, 0, tiled=True)


def wide_kernel(x, out, held, sems):
    wait(start([(x, held)], sems.at[pl.ds(4, 1)]))
    wait(start([(held, out.at[i]) for i in range(4)], sems))


def column_kernel(place, q0, q1, q2, q3, out):
    for e, q in enumerate((q0, q1, q2, q3)):
        out[lax.rem(place[1] + e, 4)] = q[...]


def panel_kernel(place, x0, x1, x2, x3, out):
    for g, x in enumerate((x0, x1, x2, x3)):
        out[lax.rem(place[3] + g, 4)] = x[...]


def start(moves, sems):
    copies = [pltpu.make_async_copy(a, b, sems.at[i]) for i, (a, b) in enumerate(moves)]
    for copy in copies:
        copy.start()
    return copies


def wait(copies):
    for copy in copies:
        copy.wait()


def first_kernel(place, own, sib, r0, r1, r2a, r2b, r3, v1, v2a, v2b, v3, keep, send, psi, right, sems):
    m, c = place[0], place[2]
    first = start([(own, psi.at[c]), (sib, psi.at[1 - c])], sems.at[3])
    slots = []
    for s in range(3):
        i, (one, low, high, three) = (s, (r1, r2a, r2b, r3)) if s < 2 else (0, (v1, v2a, v2b, v3))
        moves = [(r0.at[s], right.at[0, s]), (one.at[i], right.at[1, s]), (three.at[i], right.at[3, s])]
        moves += [(low.at[i], right.at[2, s, pl.ds(0, 256)]), (high.at[i], right.at[2, s, pl.ds(256, 256)])]
        slots.append(start(moves, sems.at[s]))
    wait(first)
    for s in range(3):
        wait(slots[s])
        for out, part in ((keep, c), (send, 1 - c)):
            total = jnp.zeros((256, 256), F32)
            for d in range(4):
                j = lax.rem(m + d, 4)
                for h in range(2):
                    rows = jnp.concatenate([psi[h, 2 * part, j], psi[h, 2 * part + 1, j]], axis=0)
                    total += jnp.dot(
                        rows, right[d, s, h * 256 : (h + 1) * 256], preferred_element_type=F32
                    )
            out[s] = total.astype(BF16)


def split(x):
    high = x.astype(BF16)
    return [high, (x - high.astype(F32)).astype(BF16)]


def second_kernel(place, left, w0, w1, w2a, w2b, w3, own, sib, out, total, l_buf, w_buf, psi, sems):
    m, l, c, live = place[0], place[1], place[2], place[4]
    slots = []
    for s in range(3):
        moves = [(left.at[:, s], l_buf.at[:, s]), (w0.at[:, s], w_buf.at[0, :, s]), (w1.at[:, s], w_buf.at[1, :, s])]
        moves += [(w2a.at[s], w_buf.at[2, 0, s]), (w2b.at[s], w_buf.at[2, 1, s]), (w3.at[:, s], w_buf.at[3, :, s])]
        slots.append(start(moves, sems.at[s]))
    last = start([(own.at[:, l], psi.at[0]), (sib.at[:, l], psi.at[1])], sems.at[3])
    for s in range(3):
        wait(slots[s])

        @pl.when(s < live)
        def _(s=s):
            for block in range(2):
                rows = slice(block * 256, (block + 1) * 256)
                for h in range(2):
                    term = jnp.zeros((256, 256), F32) if s == 0 else total[h, rows]
                    for d in range(4):
                        term += jnp.dot(
                            l_buf[lax.rem(m + d, 4), s, rows, :], w_buf[d, h, s], preferred_element_type=F32
                        )
                    total[h, rows] = term

    wait(last)
    above, below = jnp.zeros((8, 256), F32), jnp.zeros((8, 256), F32)
    for part in range(8):
        for h in range(2):
            wide = psi[h, part // 2, (part % 2) * 64 : (part % 2) * 64 + 64].astype(F32)
            term = total[h, part * 64 : (part + 1) * 64]
            above += (wide * term).reshape(8, 8, 256).sum(0)
            if h == 0:
                below += (wide * wide).reshape(8, 8, 256).sum(0)
            out[2 * part + (c if h == 0 else 1 - c), 0:64] = term.astype(BF16)
    sums = [y for x in (above, below) for y in split(x.reshape(4, 2, 256).sum(0).reshape(2, 256))]
    sums = jnp.concatenate(sums + [jnp.zeros((8, 256), BF16)], axis=0)
    for part in range(16):
        out[part, 64:80] = sums


def third_kernel(parts, out, sums):
    chunk = parts[0].astype(F32)
    for part in range(1, 16):
        chunk += parts[part].astype(F32)
    out[...] = chunk[0:64]
    for i in range(2):
        one = chunk[64 + 4 * i : 68 + 4 * i].sum(0, keepdims=True).sum(1, keepdims=True)
        sums[i : i + 1] = jnp.broadcast_to(one, (1, 128))
    sums[2:8] = jnp.zeros((6, 128), F32)


def spread_kernel(chunk, one, other, out):
    for part in range(8):
        out[part, 0:64] = chunk[...]
        out[part, 64:72, 0:128] = one[...]
        out[part, 64:72, 128:256] = other[...]


def last_kernel(parts, psi, sigma, residual, energy):
    tail = parts[0, 64:72]
    for part in range(1, 8):
        tail += parts[part, 64:72]
    tail = tail[:, 0:128] + tail[:, 128:256]
    ratio = jnp.broadcast_to(tail[0:1] / (tail[1:2] * 0.125), (8, 128))
    energy[...] = ratio
    row = jnp.concatenate([ratio[0:1], ratio[0:1]], axis=1)
    for part in range(8):
        rows = slice(part * 64, (part + 1) * 64)
        full = parts[part, 0:64]
        sigma[rows] = full.astype(BF16)
        residual[rows] = (full - row * psi[rows].astype(F32)).astype(BF16)


def call(kernel, outs, ins, *args, scratch=(), limit=8, flops=0, nbytes=1 << 10):
    return pl.pallas_call(
        kernel,
        out_shape=[jax.ShapeDtypeStruct(shape, dtype) for shape, dtype in outs],
        in_specs=ins,
        out_specs=[VMEM] * len(outs),
        scratch_shapes=scratch,
        compiler_params=pltpu.CompilerParams(vmem_limit_bytes=limit << 20),
        cost_estimate=pl.CostEstimate(flops=flops, bytes_accessed=nbytes, transcendentals=0),
    )(*args)


def per_device(psi, left_ops, right_ops_t, term_count):
    m, l, c = lax.axis_index("row"), lax.axis_index("zhi"), lax.axis_index("core")
    a = lax.axis_index("x")
    place = jnp.stack([m, l, c, a, term_count[0]]).astype(jnp.int32)


    quarter = lax.dynamic_slice_in_dim(psi, a * 128, 128, 0)
    most, last = right_ops_t[:2], right_ops_t[2:]
    r1, r3 = shift(most, "row", 4, 3), shift(most, "row", 4, 1)
    q1, q2, q3 = [shift(quarter, "zhi", 4, k) for k in (3, 2, 1)]
    wide = pl.pallas_call(
        wide_kernel,
        out_shape=jax.ShapeDtypeStruct((4, 3, 512, 256), BF16),
        in_specs=[HBM],
        out_specs=HBM,
        scratch_shapes=[pltpu.VMEM((3, 512, 256), BF16), pltpu.SemaphoreType.DMA((5,))],
        compiler_params=pltpu.CompilerParams(vmem_limit_bytes=56 << 20),
        cost_estimate=pl.CostEstimate(flops=0, bytes_accessed=1 << 10, transcendentals=0),
    )(left_ops)
    quarter, q1, q2, q3, r1, r3, last, left = together(quarter, q1, q2, q3, r1, r3, last, wide)
    left = lax.all_to_all(left, "zhi", 0, 0, tiled=True)
    v1, v3 = shift(last, "row", 4, 3), shift(last, "row", 4, 1)
    (column,) = call(column_kernel, [((4, 128, 256), BF16)], [SMEM] + [VMEM] * 4, place, quarter, q1, q2, q3)
    x1, x2, x3 = [shift(column, "x", 4, k) for k in (3, 2, 1)]
    r2a, r2b = far(r1, r3, "row", 1)
    column, x1, x2, x3, r2a, r2b, v1, v3 = together(column, x1, x2, x3, r2a, r2b, v1, v3)
    v2a, v2b = far(v1, v3, "row", 1)
    (own,) = call(panel_kernel, [((4, 4, 128, 256), BF16)], [SMEM] + [VMEM] * 4, place, column, x1, x2, x3)
    sib = shift(own, "core", 2, 1)
    keep, send = call(
        first_kernel, [((3, 256, 256), BF16)] * 2, [SMEM] + [HBM] * 11,
        place, own, sib, right_ops_t, r1, r2a, r2b, r3, v1, v2a, v2b, v3,
        scratch=[pltpu.VMEM((2, 4, 4, 128, 256), BF16), pltpu.VMEM((4, 3, 512, 256), BF16), pltpu.SemaphoreType.DMA((4, 5))],
        limit=56,
    )
    w = jnp.stack([keep, shift(send, "core", 2, 1)])
    w1, w3 = shift(w, "row", 4, 3), shift(w, "row", 4, 1)
    w2a = shift(w3[0], "row", 4, 1)
    w2b = shift(w1[1], "row", 4, 3)

    (payload,) = call(
        second_kernel, [((16, 80, 256), BF16)], [SMEM] + [HBM] * 8,
        place, left, w, w1, w2a, w2b, w3, own, sib,
        scratch=[
            pltpu.VMEM((2, 512, 256), F32), pltpu.VMEM((4, 3, 512, 256), BF16), pltpu.VMEM((4, 2, 3, 256, 256), BF16),
            pltpu.VMEM((2, 4, 128, 256), BF16), pltpu.SemaphoreType.DMA((4, 6)),
        ],
        limit=56,
    )

    parts = lax.all_to_all(payload, (*TERMS, "core"), 0, 0, tiled=True)
    chunk, sums = call(third_kernel, [((64, 256), F32), ((8, 128), F32)], [VMEM], parts)
    one = fetch(sums)
    other = shift(one, "core", 2, 1)
    (spread,) = call(spread_kernel, [((8, 72, 256), F32)], [VMEM] * 3, chunk, one, other)
    full = lax.all_to_all(spread, TERMS, 0, 0, tiled=True)
    sigma, residual, energy = call(
        last_kernel, [((512, 256), BF16), ((512, 256), BF16), ((8, 128), F32)], [VMEM] * 2, full, psi
    )
    return sigma, residual, energy[0, 0]


def solution(mesh):
    fine = Mesh(mesh.devices.reshape(4, 2, 4, 4, 2), ("x", "zlo", "row", "zhi", "core"))
    col = ("zhi", "core")
    in_specs = (P("row", col), P(TERMS, "row", col), P(TERMS, "row", col), P(TERMS))
    out_specs = (P("row", col), P("row", col), P())
    return jax.shard_map(
        per_device, mesh=fine, in_specs=in_specs, out_specs=out_specs, check_vma=False
    )
```

```python
import jax
import jax.numpy as jnp
from jax import lax
from jax.experimental import pallas as pl
from jax.experimental.pallas import tpu as pltpu
from jax.sharding import Mesh, PartitionSpec as P

TERMS = ("x", "zlo")
BF16, F32 = jnp.bfloat16, jnp.float32
SMEM = pl.BlockSpec(memory_space=pltpu.SMEM)
VMEM = pl.BlockSpec(memory_space=pltpu.VMEM)
HBM = pl.BlockSpec(memory_space=pl.ANY)


def shift(x, axis, n, k):
    return lax.ppermute(x, axis, [(i, (i + k) % n) for i in range(n)])


def together(*xs):
    return lax.optimization_barrier(xs)


def far(after, before, axis, dim):
    half = after.shape[dim] // 2
    low = shift(lax.slice_in_dim(before, 0, half, axis=dim), axis, 4, 1)
    high = shift(lax.slice_in_dim(after, half, 2 * half, axis=dim), axis, 4, 3)
    return low, high


def spread_to(x, axis):
    n = 4
    return lax.all_to_all(jnp.broadcast_to(x[None], (n, *x.shape)), axis, 0, 0, tiled=True)


def wide_kernel(x, out, held, sems):
    wait(start([(x, held)], sems.at[pl.ds(4, 1)]))
    wait(start([(held, out.at[i]) for i in range(4)], sems))


def column_kernel(place, q0, q1, q2, q3, out):
    for e, q in enumerate((q0, q1, q2, q3)):
        out[lax.rem(place[1] + e, 4)] = q[...]


def panel_kernel(place, x0, x1, x2, x3, out):
    for g, x in enumerate((x0, x1, x2, x3)):
        out[lax.rem(place[3] + g, 4)] = x[...]


def start(moves, sems):
    copies = [pltpu.make_async_copy(a, b, sems.at[i]) for i, (a, b) in enumerate(moves)]
    for copy in copies:
        copy.start()
    return copies


def wait(copies):
    for copy in copies:
        copy.wait()


def first_kernel(place, own, sib, r0, r1, r2a, r2b, r3, v1, v2a, v2b, v3, keep, send, psi, right, sems):
    m, c = place[0], place[2]
    first = start([(own, psi.at[c]), (sib, psi.at[1 - c])], sems.at[3])
    slots = []
    for s in range(3):
        i, (one, low, high, three) = (s, (r1, r2a, r2b, r3)) if s < 2 else (0, (v1, v2a, v2b, v3))
        moves = [(r0.at[s], right.at[0, s]), (one.at[i], right.at[1, s]), (three.at[i], right.at[3, s])]
        moves += [(low.at[i], right.at[2, s, pl.ds(0, 256)]), (high.at[i], right.at[2, s, pl.ds(256, 256)])]
        slots.append(start(moves, sems.at[s]))
    wait(first)
    for s in range(3):
        wait(slots[s])
        for out, part in ((keep, c), (send, 1 - c)):
            total = jnp.zeros((256, 256), F32)
            for d in range(4):
                j = lax.rem(m + d, 4)
                for h in range(2):
                    rows = jnp.concatenate([psi[h, 2 * part, j], psi[h, 2 * part + 1, j]], axis=0)
                    total += jnp.dot(
                        rows, right[d, s, h * 256 : (h + 1) * 256], preferred_element_type=F32
                    )
            out[s] = total.astype(BF16)


def split(x):
    high = x.astype(BF16)
    return [high, (x - high.astype(F32)).astype(BF16)]


def second_kernel(place, left, w0, w1, w2a, w2b, w3, own, sib, out, total, l_buf, w_buf, psi, sems):
    m, l, c, live = place[0], place[1], place[2], place[4]
    slots = []
    for s in range(3):
        moves = [(left.at[:, s], l_buf.at[:, s]), (w0.at[:, s], w_buf.at[0, :, s]), (w1.at[:, s], w_buf.at[1, :, s])]
        moves += [(w2a.at[s], w_buf.at[2, 0, s]), (w2b.at[s], w_buf.at[2, 1, s]), (w3.at[:, s], w_buf.at[3, :, s])]
        slots.append(start(moves, sems.at[s]))
    last = start([(own.at[:, l], psi.at[0]), (sib.at[:, l], psi.at[1])], sems.at[3])
    for s in range(3):
        wait(slots[s])

        @pl.when(s < live)
        def _(s=s):
            for block in range(2):
                rows = slice(block * 256, (block + 1) * 256)
                for h in range(2):
                    term = jnp.zeros((256, 256), F32) if s == 0 else total[h, rows]
                    for d in range(4):
                        term += jnp.dot(
                            l_buf[lax.rem(m + d, 4), s, rows, :], w_buf[d, h, s], preferred_element_type=F32
                        )
                    total[h, rows] = term

    wait(last)
    above, below = jnp.zeros((8, 256), F32), jnp.zeros((8, 256), F32)
    for part in range(8):
        for h in range(2):
            wide = psi[h, part // 2, (part % 2) * 64 : (part % 2) * 64 + 64].astype(F32)
            term = total[h, part * 64 : (part + 1) * 64]
            above += (wide * term).reshape(8, 8, 256).sum(0)
            if h == 0:
                below += (wide * wide).reshape(8, 8, 256).sum(0)
            out[2 * part + (c if h == 0 else 1 - c), 0:64] = term.astype(BF16)
    sums = [y for x in (above, below) for y in split(x.reshape(4, 2, 256).sum(0).reshape(2, 256))]
    sums = jnp.concatenate(sums + [jnp.zeros((8, 256), BF16)], axis=0)
    for part in range(16):
        out[part, 64:80] = sums


def third_kernel(parts, out, sums):
    chunk = parts[0].astype(F32)
    for part in range(1, 16):
        chunk += parts[part].astype(F32)
    for part in range(8):
        out[part] = chunk[0:64]
    for i in range(2):
        one = chunk[64 + 4 * i : 68 + 4 * i].sum(0, keepdims=True).sum(1, keepdims=True)
        sums[i : i + 1] = jnp.broadcast_to(one, (1, 128))
    sums[2:8] = jnp.zeros((6, 128), F32)


def last_kernel(parts, sums, psi, sigma, residual, energy):
    ratio = jnp.broadcast_to(sums[0:1] / (sums[1:2] * 0.125), (8, 128))
    energy[...] = ratio[0:1, 0:1]
    row = jnp.concatenate([ratio[0:1], ratio[0:1]], axis=1)
    for part in range(8):
        rows = slice(part * 64, (part + 1) * 64)
        full = parts[part]
        sigma[rows] = full.astype(BF16)
        residual[rows] = (full - row * psi[rows].astype(F32)).astype(BF16)


def call(kernel, outs, ins, *args, scratch=(), limit=8, flops=0, nbytes=1 << 10):
    return pl.pallas_call(
        kernel,
        out_shape=[jax.ShapeDtypeStruct(shape, dtype) for shape, dtype in outs],
        in_specs=ins,
        out_specs=[VMEM] * len(outs),
        scratch_shapes=scratch,
        compiler_params=pltpu.CompilerParams(vmem_limit_bytes=limit << 20),
        cost_estimate=pl.CostEstimate(flops=flops, bytes_accessed=nbytes, transcendentals=0),
    )(*args)


def per_device(psi, left_ops, right_ops_t, term_count):
    m, l, c = lax.axis_index("row"), lax.axis_index("zhi"), lax.axis_index("core")
    a = lax.axis_index("x")
    place = jnp.stack([m, l, c, a, term_count[0]]).astype(jnp.int32)


    quarter = lax.dynamic_slice_in_dim(psi, a * 128, 128, 0)
    most, last = right_ops_t[:2], right_ops_t[2:]
    r1, r3 = shift(most, "row", 4, 3), shift(most, "row", 4, 1)
    q1, q2, q3 = [shift(quarter, "zhi", 4, k) for k in (3, 2, 1)]
    wide = pl.pallas_call(
        wide_kernel,
        out_shape=jax.ShapeDtypeStruct((4, 3, 512, 256), BF16),
        in_specs=[HBM],
        out_specs=HBM,
        scratch_shapes=[pltpu.VMEM((3, 512, 256), BF16), pltpu.SemaphoreType.DMA((5,))],
        compiler_params=pltpu.CompilerParams(vmem_limit_bytes=56 << 20),
        cost_estimate=pl.CostEstimate(flops=0, bytes_accessed=1 << 10, transcendentals=0),
    )(left_ops)
    quarter, q1, q2, q3, r1, r3, last, left = together(quarter, q1, q2, q3, r1, r3, last, wide)
    left = lax.all_to_all(left, "zhi", 0, 0, tiled=True)
    v1, v3 = shift(last, "row", 4, 3), shift(last, "row", 4, 1)
    (column,) = call(column_kernel, [((4, 128, 256), BF16)], [SMEM] + [VMEM] * 4, place, quarter, q1, q2, q3)
    x1, x2, x3 = [shift(column, "x", 4, k) for k in (3, 2, 1)]
    r2a, r2b = far(r1, r3, "row", 1)
    column, x1, x2, x3, r2a, r2b, v1, v3 = together(column, x1, x2, x3, r2a, r2b, v1, v3)
    v2a, v2b = far(v1, v3, "row", 1)
    (own,) = call(panel_kernel, [((4, 4, 128, 256), BF16)], [SMEM] + [VMEM] * 4, place, column, x1, x2, x3)
    sib = shift(own, "core", 2, 1)
    keep, send = call(
        first_kernel, [((3, 256, 256), BF16)] * 2, [SMEM] + [HBM] * 11,
        place, own, sib, right_ops_t, r1, r2a, r2b, r3, v1, v2a, v2b, v3,
        scratch=[pltpu.VMEM((2, 4, 4, 128, 256), BF16), pltpu.VMEM((4, 3, 512, 256), BF16), pltpu.SemaphoreType.DMA((4, 5))],
        limit=56,
    )
    w = jnp.stack([keep, shift(send, "core", 2, 1)])
    w1, w3 = shift(w, "row", 4, 3), shift(w, "row", 4, 1)
    w2a = shift(w3[0], "row", 4, 1)
    w2b = shift(w1[1], "row", 4, 3)

    (payload,) = call(
        second_kernel, [((16, 80, 256), BF16)], [SMEM] + [HBM] * 8,
        place, left, w, w1, w2a, w2b, w3, own, sib,
        scratch=[
            pltpu.VMEM((2, 512, 256), F32), pltpu.VMEM((4, 3, 512, 256), BF16), pltpu.VMEM((4, 2, 3, 256, 256), BF16),
            pltpu.VMEM((2, 4, 128, 256), BF16), pltpu.SemaphoreType.DMA((4, 6)),
        ],
        limit=56,
    )

    parts = lax.all_to_all(payload, (*TERMS, "core"), 0, 0, tiled=True)
    chunk, sums = call(third_kernel, [((8, 64, 256), F32), ((8, 128), F32)], [VMEM], parts)
    full = lax.all_to_all(chunk, TERMS, 0, 0, tiled=True)
    for axis in ("row", "zhi"):
        sums = sums + shift(sums, axis, 4, 1) + shift(sums, axis, 4, 2) + shift(sums, axis, 4, 3)
    sigma, residual, energy = call(
        last_kernel, [((512, 256), BF16), ((512, 256), BF16), ((1, 1), F32)], [VMEM] * 3, full, sums, psi
    )
    return sigma, residual, energy.reshape(())


def solution(mesh):
    fine = Mesh(mesh.devices.reshape(4, 2, 4, 4, 2), ("x", "zlo", "row", "zhi", "core"))
    col = ("zhi", "core")
    in_specs = (P("row", col), P(TERMS, "row", col), P(TERMS, "row", col), P(TERMS))
    out_specs = (P("row", col), P("row", col), P())
    return jax.shard_map(
        per_device, mesh=fine, in_specs=in_specs, out_specs=out_specs, check_vma=False
    )
```

```python
import jax
import jax.numpy as jnp
from jax import lax
from jax.experimental import pallas as pl
from jax.experimental.pallas import tpu as pltpu
from jax.sharding import Mesh, PartitionSpec as P

TERMS = ("x", "zlo")
BF16, F32 = jnp.bfloat16, jnp.float32
SMEM = pl.BlockSpec(memory_space=pltpu.SMEM)
VMEM = pl.BlockSpec(memory_space=pltpu.VMEM)
HBM = pl.BlockSpec(memory_space=pl.ANY)


def shift(x, axis, n, k):
    return lax.ppermute(x, axis, [(i, (i + k) % n) for i in range(n)])


def together(*xs):
    return lax.optimization_barrier(xs)


def far(after, before, axis, dim):
    half = after.shape[dim] // 2
    low = shift(lax.slice_in_dim(before, 0, half, axis=dim), axis, 4, 1)
    high = shift(lax.slice_in_dim(after, half, 2 * half, axis=dim), axis, 4, 3)
    return low, high


def spread_to(x, axis):
    n = 4
    return lax.all_to_all(jnp.broadcast_to(x[None], (n, *x.shape)), axis, 0, 0, tiled=True)


def wide_kernel(x, out, held, sems):
    wait(start([(x, held)], sems.at[pl.ds(4, 1)]))
    wait(start([(held, out.at[i]) for i in range(4)], sems))


def column_kernel(place, q0, q1, q2, q3, out):
    for e, q in enumerate((q0, q1, q2, q3)):
        out[lax.rem(place[1] + e, 4)] = q[...]


def panel_kernel(place, x0, x1, x2, x3, out):
    for g, x in enumerate((x0, x1, x2, x3)):
        out[lax.rem(place[3] + g, 4)] = x[...]


def start(moves, sems):
    copies = [pltpu.make_async_copy(a, b, sems.at[i]) for i, (a, b) in enumerate(moves)]
    for copy in copies:
        copy.start()
    return copies


def wait(copies):
    for copy in copies:
        copy.wait()


def first_kernel(place, own, sib, r0, r1, r2a, r2b, r3, v1, v2a, v2b, v3, keep, send, psi, right, sems):
    m, c = place[0], place[2]
    first = start([(own, psi.at[c]), (sib, psi.at[1 - c])], sems.at[3])
    slots = []
    for s in range(3):
        i, (one, low, high, three) = (s, (r1, r2a, r2b, r3)) if s < 2 else (0, (v1, v2a, v2b, v3))
        moves = [(r0.at[s], right.at[0, s]), (one.at[i], right.at[1, s]), (three.at[i], right.at[3, s])]
        moves += [(low.at[i], right.at[2, s, pl.ds(0, 256)]), (high.at[i], right.at[2, s, pl.ds(256, 256)])]
        slots.append(start(moves, sems.at[s]))
    wait(first)
    for s in range(3):
        wait(slots[s])
        for out, part in ((keep, c), (send, 1 - c)):
            total = jnp.zeros((256, 256), F32)
            for d in range(4):
                j = lax.rem(m + d, 4)
                for h in range(2):
                    rows = jnp.concatenate([psi[h, 2 * part, j], psi[h, 2 * part + 1, j]], axis=0)
                    total += jnp.dot(
                        rows, right[d, s, h * 256 : (h + 1) * 256], preferred_element_type=F32
                    )
            out[s] = total.astype(BF16)


def split(x):
    high = x.astype(BF16)
    return [high, (x - high.astype(F32)).astype(BF16)]


def second_kernel(place, left, w0, w1, w2a, w2b, w3, own, sib, out, total, l_buf, w_buf, psi, sems):
    m, l, c, live = place[0], place[1], place[2], place[4]
    slots = []
    for s in range(3):
        moves = [(left.at[:, s], l_buf.at[:, s]), (w0.at[:, s], w_buf.at[0, :, s]), (w1.at[:, s], w_buf.at[1, :, s])]
        moves += [(w2a.at[s], w_buf.at[2, 0, s]), (w2b.at[s], w_buf.at[2, 1, s]), (w3.at[:, s], w_buf.at[3, :, s])]
        slots.append(start(moves, sems.at[s]))
    last = start([(own.at[:, l], psi.at[0]), (sib.at[:, l], psi.at[1])], sems.at[3])
    for s in range(3):
        wait(slots[s])

        @pl.when(s < live)
        def _(s=s):
            for block in range(2):
                rows = slice(block * 256, (block + 1) * 256)
                for h in range(2):
                    term = jnp.zeros((256, 256), F32) if s == 0 else total[h, rows]
                    for d in range(4):
                        term += jnp.dot(
                            l_buf[lax.rem(m + d, 4), s, rows, :], w_buf[d, h, s], preferred_element_type=F32
                        )
                    total[h, rows] = term

    wait(last)
    above, below = jnp.zeros((8, 256), F32), jnp.zeros((8, 256), F32)
    for part in range(8):
        for h in range(2):
            wide = psi[h, part // 2, (part % 2) * 64 : (part % 2) * 64 + 64].astype(F32)
            term = total[h, part * 64 : (part + 1) * 64]
            above += (wide * term).reshape(8, 8, 256).sum(0)
            if h == 0:
                below += (wide * wide).reshape(8, 8, 256).sum(0)
            out[2 * part + (c if h == 0 else 1 - c), 0:64] = term.astype(BF16)
    sums = [y for x in (above, below) for y in split(x.reshape(4, 2, 256).sum(0).reshape(2, 256))]
    sums = jnp.concatenate(sums + [jnp.zeros((8, 256), BF16)], axis=0)
    for part in range(16):
        out[part, 64:80] = sums


def third_kernel(parts, out, sums):
    chunk = parts[0].astype(F32)
    for part in range(1, 16):
        chunk += parts[part].astype(F32)
    for part in range(8):
        out[part] = chunk[0:64]
    for i in range(2):
        one = chunk[64 + 4 * i : 68 + 4 * i].sum(0, keepdims=True).sum(1, keepdims=True)
        sums[i : i + 1] = jnp.broadcast_to(one, (1, 128))
    sums[2:8] = jnp.zeros((6, 128), F32)


def last_kernel(parts, sums, psi, sigma, residual, energy):
    ratio = jnp.broadcast_to(sums[0:1] / (sums[1:2] * 0.125), (8, 128))
    energy[...] = ratio[0:1, 0:1]
    row = jnp.concatenate([ratio[0:1], ratio[0:1]], axis=1)
    for part in range(8):
        rows = slice(part * 64, (part + 1) * 64)
        full = parts[part]
        sigma[rows] = full.astype(BF16)
        residual[rows] = (full - row * psi[rows].astype(F32)).astype(BF16)


def call(kernel, outs, ins, *args, scratch=(), limit=8, flops=0, nbytes=1 << 10):
    return pl.pallas_call(
        kernel,
        out_shape=[jax.ShapeDtypeStruct(shape, dtype) for shape, dtype in outs],
        in_specs=ins,
        out_specs=[VMEM] * len(outs),
        scratch_shapes=scratch,
        compiler_params=pltpu.CompilerParams(vmem_limit_bytes=limit << 20),
        cost_estimate=pl.CostEstimate(flops=flops, bytes_accessed=nbytes, transcendentals=0),
    )(*args)


def per_device(psi, left_ops, right_ops_t, term_count):
    m, l, c = lax.axis_index("row"), lax.axis_index("zhi"), lax.axis_index("core")
    a = lax.axis_index("x")
    place = jnp.stack([m, l, c, a, term_count[0]]).astype(jnp.int32)


    quarter = lax.dynamic_slice_in_dim(psi, a * 128, 128, 0)
    most, last = right_ops_t[:2], right_ops_t[2:]
    r1, r3 = shift(most, "row", 4, 3), shift(most, "row", 4, 1)
    q1, q2, q3 = [shift(quarter, "zhi", 4, k) for k in (3, 2, 1)]
    wide = pl.pallas_call(
        wide_kernel,
        out_shape=jax.ShapeDtypeStruct((4, 3, 512, 256), BF16),
        in_specs=[HBM],
        out_specs=HBM,
        scratch_shapes=[pltpu.VMEM((3, 512, 256), BF16), pltpu.SemaphoreType.DMA((5,))],
        compiler_params=pltpu.CompilerParams(vmem_limit_bytes=56 << 20),
        cost_estimate=pl.CostEstimate(flops=0, bytes_accessed=1 << 10, transcendentals=0),
    )(left_ops)
    quarter, q1, q2, q3, r1, r3, last, left = together(quarter, q1, q2, q3, r1, r3, last, wide)
    left = lax.all_to_all(left, "zhi", 0, 0, tiled=True)
    v1, v3 = shift(last, "row", 4, 3), shift(last, "row", 4, 1)
    (column,) = call(column_kernel, [((4, 128, 256), BF16)], [SMEM] + [VMEM] * 4, place, quarter, q1, q2, q3)
    x1, x2, x3 = [shift(column, "x", 4, k) for k in (3, 2, 1)]
    r2a, r2b = far(r1, r3, "row", 1)
    column, x1, x2, x3, r2a, r2b, v1, v3 = together(column, x1, x2, x3, r2a, r2b, v1, v3)
    v2a, v2b = far(v1, v3, "row", 1)
    (own,) = call(panel_kernel, [((4, 4, 128, 256), BF16)], [SMEM] + [VMEM] * 4, place, column, x1, x2, x3)
    sib = shift(own, "core", 2, 1)
    keep, send = call(
        first_kernel, [((3, 256, 256), BF16)] * 2, [SMEM] + [HBM] * 11,
        place, own, sib, right_ops_t, r1, r2a, r2b, r3, v1, v2a, v2b, v3,
        scratch=[pltpu.VMEM((2, 4, 4, 128, 256), BF16), pltpu.VMEM((4, 3, 512, 256), BF16), pltpu.SemaphoreType.DMA((4, 5))],
        limit=56,
    )
    w = jnp.stack([keep, shift(send, "core", 2, 1)])
    w1, w3 = shift(w, "row", 4, 3), shift(w, "row", 4, 1)
    w2a = shift(w3[0], "row", 4, 1)
    w2b = shift(w1[1], "row", 4, 3)

    (payload,) = call(
        second_kernel, [((16, 80, 256), BF16)], [SMEM] + [HBM] * 8,
        place, left, w, w1, w2a, w2b, w3, own, sib,
        scratch=[
            pltpu.VMEM((2, 512, 256), F32), pltpu.VMEM((4, 3, 512, 256), BF16), pltpu.VMEM((4, 2, 3, 256, 256), BF16),
            pltpu.VMEM((2, 4, 128, 256), BF16), pltpu.SemaphoreType.DMA((4, 6)),
        ],
        limit=56,
    )

    parts = lax.all_to_all(payload, (*TERMS, "core"), 0, 0, tiled=True)
    chunk, sums = call(third_kernel, [((8, 64, 256), F32), ((8, 128), F32)], [VMEM], parts)
    full = lax.all_to_all(chunk, TERMS, 0, 0, tiled=True)
    sums = sums + shift(sums, "row", 4, 1) + shift(sums, "row", 4, 2) + shift(sums, "row", 4, 3)
    for k in (1, 2):
        sums = sums + lax.ppermute(sums, "zhi", [(i, i ^ k) for i in range(4)])
    sigma, residual, energy = call(
        last_kernel, [((512, 256), BF16), ((512, 256), BF16), ((1, 1), F32)], [VMEM] * 3, full, sums, psi
    )
    return sigma, residual, energy.reshape(())


def solution(mesh):
    fine = Mesh(mesh.devices.reshape(4, 2, 4, 4, 2), ("x", "zlo", "row", "zhi", "core"))
    col = ("zhi", "core")
    in_specs = (P("row", col), P(TERMS, "row", col), P(TERMS, "row", col), P(TERMS))
    out_specs = (P("row", col), P("row", col), P())
    return jax.shard_map(
        per_device, mesh=fine, in_specs=in_specs, out_specs=out_specs, check_vma=False
    )
```
